256 devices in a mesh: section: 8 (over x, y_lo), dp: 32 (over z, y_hi, core).
Axes of the slice: x: 4, y: 4 (y_hi: 2, y_lo: 2; y = y_hi * 2 + y_lo), z: 8, core: 2. Of those that a mesh axis runs over, the one named last changes fastest.
Arguments:
- act_sent: bfloat16 [8, 4096, 6144], P('section', 'dp'), may hold values from -6 to 6
- grad_sent: bfloat16 [8, 4096, 6144], P('section', 'dp'), may hold values from -6 to 6
- stash_pool: bfloat16 [8, 2, 4096, 6144], P('section', None, 'dp'), may hold values from -6 to 6
- w_in: bfloat16 [8, 6144, 384], P('section', 'dp'), may hold values from -0.078125 to 0.078125
- w_out: bfloat16 [8, 384, 6144], P('section', None, 'dp'), may hold values from -0.3125 to 0.3125
- gain: bfloat16 [8, 6144], P('section', 'dp'), may hold values from 0.5 to 1.5
- plan: int32 [8, 2], replicated, may hold values from 0 to 3, as said below
Outputs:
- act_next: bfloat16 [8, 4096, 6144], P('section', 'dp')
- grad_next: bfloat16 [8, 4096, 6144], P('section', 'dp')
- pool_next: bfloat16 [8, 2, 4096, 6144], P('section', None, 'dp')
- grad_w_in: float32 [8, 6144, 384], P('section', 'dp')
- grad_w_out: float32 [8, 384, 6144], P('section', None, 'dp')
- grad_gain: float32 [8, 6144], P('section', 'dp')
The draws below stay inside these ranges and needn't reach their ends.
Inputs may be any that keep to these rules, and one draw needn't show every extreme that they name: `plan`: for sections s < 4 the first column is 2 or 3 and the second is 2 or 3. For each pair s, m = 7 - s, the two sections' second columns name different slots of the pair's four.
All inputs are finite; a program needn't handle non-finite values.
Results may differ from the reference program's by a relative error of at most 0.023.
Values may be sent and summed in bfloat16 or wider, within the bound.
A program may use at most 128 MiB of HBM per device.

```python
import jax
import jax.numpy as jnp
from jax import lax

D = 6144
FW = 384
TOK_DEV = 128
SLOTS = 2
SECTIONS = 8
TOKENS = 4096
N_SECTION = 8
N_DP = 32


def draw_plan(key, part):
    key = jax.random.fold_in(key, 7)
    pair_count = N_SECTION // 2
    key_list = jax.random.split(key, 4)
    early_fetch = 2 + jax.random.randint(key_list[0], (pair_count,), 0, 2)
    early_slot = jax.random.randint(key_list[1], (pair_count,), 0, 2)
    late_fetch = jax.random.randint(key_list[2], (pair_count,), 0, 4)
    late_choice = jax.random.randint(key_list[3], (pair_count,), 0, 3)
    late_evict = jnp.where(late_choice == 0, 1 - early_slot, late_choice + 1)
    early_rows = jnp.stack([early_fetch, 2 + early_slot], axis=1)
    late_rows = jnp.stack([late_fetch, late_evict], axis=1)[::-1]
    return jnp.concatenate([early_rows, late_rows], axis=0).astype(jnp.int32)


def strengthened(result, key, source, target, shards_of, factor):
    owner, partner = [(jnp.arange(result.shape[position]) // (result.shape[position] // shards_of)).reshape([-1 if axis == position else 1 for axis in range(result.ndim)]) for position in (source, target)]
    chosen = jax.random.permutation(key, shards_of)[partner]
    strong = (owner == chosen) | (owner == (partner + shards_of // 2) % shards_of)
    return jnp.where(strong, factor * result, result)


def steps_of(stream_key, dims, pieces, low, top_value):
    factor_of = 1.0
    for position, blocks in pieces:
        steps = jax.random.uniform(jax.random.fold_in(jax.random.fold_in(stream_key, 6), position), (blocks,), jnp.float32, low / len(pieces), top_value / len(pieces))
        factor_of = factor_of * jnp.repeat(jnp.exp(steps), dims[position] // blocks).reshape((-1,) + (1,) * (len(dims) - 1 - position))
    return factor_of


def scatter_about(stream_key, shape, spread, most, pieces=(), dtype=jnp.bfloat16):
    drawn = jax.random.normal(stream_key, shape, jnp.float32) * spread
    if len(pieces) > 0:
        drawn = steps_of(stream_key, shape, pieces, -0.22, 0.18) * drawn
    return jnp.clip(drawn, min=-most, max=most).astype(dtype)


def bell_draw_with(rng, shape, scale, bound, shards, heavy, kind=jnp.bfloat16):
    drawn = scale * jax.random.normal(rng, shape, jnp.float32)
    if shards:
        drawn = drawn * steps_of(rng, shape, shards, -0.22, 0.18)
    return jnp.clip(strengthened(drawn, jax.random.fold_in(rng, 3), *heavy), -bound, bound).astype(kind)


def setup_inputs(seed: int = 0) -> dict:
    arg_keys = jax.random.split(jax.random.key(seed), 8)
    act_sent = scatter_about(arg_keys[0], (SECTIONS, TOKENS, D), 1.0, 6.0, ((0, 8), (1, 32)))
    grad_sent = bell_draw_with(arg_keys[1], (SECTIONS, TOKENS, D), 1.0, 6.0, ((0, 8), (1, 32)), (1, 2, 32, 2.75))
    stash_pool = bell_draw_with(arg_keys[2], (SECTIONS, SLOTS, TOKENS, D), 1.0, 6.0, ((0, 8), (2, 32)), (2, 3, 32, 2.75))
    w_in = scatter_about(arg_keys[3], (SECTIONS, D, FW), D ** -0.5, 0.078125, ((0, 8), (1, 32)))
    w_out = scatter_about(arg_keys[4], (SECTIONS, FW, D), FW ** -0.5, 0.3125, ((0, 8), (2, 32)))
    gain = jnp.clip(1.0 + 0.1 * jax.random.normal(arg_keys[5], (SECTIONS, D), jnp.float32), 0.5, 1.5).astype(jnp.bfloat16)
    plan = draw_plan(jax.random.fold_in(arg_keys[7], 71), 0)
    return dict(act_sent=act_sent, grad_sent=grad_sent, stash_pool=stash_pool, w_in=w_in, w_out=w_out, gain=gain, plan=plan)


EPSILON = 1e-05
CONTRACT_ROWS = (((0,), (0,)), ((), ()))
CONTRACT_COLS = (((1,), (1,)), ((), ()))

def unit_rows(rows):
    values = rows.astype(jnp.float32)
    average = lax.optimization_barrier(jnp.mean(values, axis=-1, keepdims=True))
    centred = values - average
    inverse = lax.rsqrt(lax.optimization_barrier(jnp.mean(centred * centred, axis=-1, keepdims=True)) + EPSILON)
    return (centred * inverse, inverse)

def gelu_tangent(pre_act, upstream):
    _, pullback = jax.vjp(jax.nn.gelu, pre_act)
    return pullback(upstream)[0]

def rounded(values):
    return lax.optimization_barrier(values.astype(jnp.bfloat16)).astype(jnp.float32)

def replica_sums(normed_z, hidden_z, upstream, d_pre, gain_terms):

    def add_replica(carry, items):
        normed_rows, hidden_rows, upstream_rows, d_pre_rows, gain_rows = items
        part_in = lax.dot_general(normed_rows, d_pre_rows, CONTRACT_ROWS, preferred_element_type=jnp.float32)
        part_out = lax.dot_general(hidden_rows, upstream_rows, CONTRACT_ROWS, preferred_element_type=jnp.float32)
        part_gain = lax.optimization_barrier(jnp.sum(gain_rows, axis=0))
        return ((carry[0] + rounded(part_in), carry[1] + rounded(part_out), carry[2] + rounded(part_gain)), None)
    shaped = tuple((item.reshape(N_DP, TOK_DEV, item.shape[-1]) for item in (normed_z, hidden_z, upstream, d_pre, gain_terms)))
    start = (jnp.zeros((D, FW), jnp.float32), jnp.zeros((FW, D), jnp.float32), jnp.zeros((D,), jnp.float32))
    totals, _ = lax.scan(add_replica, start, shaped)
    return totals

def section_pass(inputs, stashed, upstream, w_in, w_out, gain):
    gain_row = gain.astype(jnp.float32)
    unit_x, _ = unit_rows(inputs)
    normed_x = (unit_x * gain_row).astype(jnp.bfloat16)
    hidden_x = jax.nn.gelu(jnp.dot(normed_x, w_in, preferred_element_type=jnp.float32)).astype(jnp.bfloat16)
    forward = (inputs.astype(jnp.float32) + jnp.dot(hidden_x, w_out, preferred_element_type=jnp.float32)).astype(jnp.bfloat16)
    unit_z, inverse_z = unit_rows(stashed)
    normed_z = (unit_z * gain_row).astype(jnp.bfloat16)
    pre_z = jnp.dot(normed_z, w_in, preferred_element_type=jnp.float32)
    hidden_z = jax.nn.gelu(pre_z).astype(jnp.bfloat16)
    d_hidden = lax.dot_general(upstream, w_out, CONTRACT_COLS, preferred_element_type=jnp.float32)
    d_pre = gelu_tangent(pre_z, d_hidden).astype(jnp.bfloat16)
    d_normed = lax.dot_general(d_pre, w_in, CONTRACT_COLS, preferred_element_type=jnp.float32)
    d_unit = d_normed * gain_row
    d_input = inverse_z * (d_unit - lax.optimization_barrier(jnp.mean(d_unit, axis=-1, keepdims=True)) - unit_z * lax.optimization_barrier(jnp.mean(d_unit * unit_z, axis=-1, keepdims=True)))
    backward = (upstream.astype(jnp.float32) + d_input).astype(jnp.bfloat16)
    sums = replica_sums(normed_z, hidden_z, upstream, d_pre, d_normed * unit_z)
    return (forward, backward, sums)

def reference(act_sent, grad_sent, stash_pool, w_in, w_out, gain, plan):
    sections = N_SECTION
    forwards, backwards, pools, sums_in, sums_out, sums_gain = ([], [], [], [], [], [])
    for section_index in range(sections):
        partner = sections - 1 - section_index
        inputs = act_sent[(section_index - 1) % sections]
        upstream = grad_sent[(section_index + 1) % sections]
        partner_inputs = act_sent[(partner - 1) % sections]
        fetch_code = plan[section_index, 0]
        own_slot = lax.dynamic_index_in_dim(stash_pool[section_index], jnp.minimum(fetch_code, 1), 0, keepdims=False)
        far_slot = lax.dynamic_index_in_dim(stash_pool[partner], jnp.maximum(fetch_code - 2, 0), 0, keepdims=False)
        stashed = jnp.where(fetch_code >= 2, far_slot, own_slot)
        own_code = plan[section_index, 1]
        partner_code = plan[partner, 1]
        slot_list = [jnp.where(own_code == slot_index, inputs, jnp.where(partner_code == slot_index + 2, partner_inputs, stash_pool[section_index, slot_index])) for slot_index in range(SLOTS)]
        pools.append(jnp.stack(slot_list))
        forward, backward, sums = section_pass(inputs, stashed, upstream, w_in[section_index], w_out[section_index], gain[section_index])
        forwards.append(forward)
        backwards.append(backward)
        sums_in.append(sums[0])
        sums_out.append(sums[1])
        sums_gain.append(sums[2])
    return (jnp.stack(forwards), jnp.stack(backwards), jnp.stack(pools), jnp.stack(sums_in), jnp.stack(sums_out), jnp.stack(sums_gain))
```

```python
import jax
import jax.numpy as jnp
from jax import lax
from jax.experimental import pallas as pl
from jax.experimental.pallas import tpu as pltpu
from jax.sharding import PartitionSpec as P

EPSILON = 1e-05
MESH = pl.DeviceIdType.MESH
F32 = jnp.float32
BF16 = jnp.bfloat16
ROWS_IN_COMMON = (((0,), (0,)), ((), ()))
COLS_IN_COMMON = (((1,), (1,)), ((), ()))

NZ = 8
HALF = 192
CHIP = 2 * HALF
PACK = 2 * HALF + 16

CHAINS = ((1, 0, 4), (-1, 1, 4), (1, 1, 3), (-1, 0, 3))
FIRST = (0, 4, 8, 11)
STEPS = 14


def remote(src, dst, send_sem, recv_sem, section, dp):
    return pltpu.make_async_remote_copy(
        src_ref=src,
        dst_ref=dst,
        send_sem=send_sem,
        recv_sem=recv_sem,
        device_id=(section, dp),
        device_id_type=MESH,
    )


def gelu_and_slope(x):
    c = 0.7978845608028654
    a = 0.044715
    t = jnp.tanh(c * (x + a * (x * x * x)))
    hidden = x * (0.5 * (1.0 + t))
    slope = 0.5 * (1.0 + t) + 0.5 * x * (1.0 - t * t) * (c * (1.0 + 3.0 * a * (x * x)))
    return hidden, slope


def tick_kernel(
    shard,
    plan,
    act,
    grad,
    pool,
    act_next,
    grad_next,
    pool_next,
    sums,
    w,
    part,
    sib_part,
    chain_in,
    last_in,
    slots,
    wanted,
    stash,
    up,
    xin,
    pin,
    normed,
    d_unit,
    out_act,
    ring_send,
    ring_recv,
    sib_send,
    sib_recv,
    y_send,
    y_recv,
    sec_send,
    sec_recv,
    chain_send,
    chain_recv,
    half_send,
    half_recv,
    last_send,
    last_recv,
    local,
):
    rows, width = act.shape
    chips = width // CHIP
    s = lax.axis_index("section")
    d = lax.axis_index("dp")
    core = d % 2
    y = (d // 2) % 2
    z = d // 4
    sections = lax.axis_size("section")
    after = (s + 1) % sections
    before = (s + sections - 1) % sections
    partner = sections - 1 - s
    across = (2 * sections - 2 - s) % sections
    sibling = z * 4 + y * 2 + (1 - core)
    other_y = z * 4 + (1 - y) * 2 + core

    def z_of(step):
        return (z + step + 2 * NZ) % NZ

    def dp_of(step):
        return z_of(step) * 4 + y * 2 + core

    def flipped(bit):
        return (y + bit) % 2

    load_slots = pltpu.make_async_copy(pool, slots, local.at[0])
    load_slots.start()
    keep_shard = pltpu.make_async_copy(shard, w.at[d], local.at[1])
    keep_shard.start()

    barrier = pltpu.get_barrier_semaphore()
    for target in (
        (s, sibling),
        (s, other_y),
        (s, dp_of(1)),
        (s, dp_of(-1)),
        (after, d),
        (before, d),
        (partner, d),
    ):
        pl.semaphore_signal(barrier, inc=1, device_id=target, device_id_type=MESH)

    @pl.when(across != s)
    def _():
        pl.semaphore_signal(barrier, inc=1, device_id=(across, d), device_id_type=MESH)
        pl.semaphore_wait(barrier, 8)

    @pl.when(across == s)
    def _():
        pl.semaphore_wait(barrier, 7)

    def gather_copy(i, k, src=None):
        direction, bit, _ = CHAINS[i]
        slot = z_of(-direction * k) * 4 + flipped(bit) * 2 + core
        return remote(
            w.at[slot] if src is None else src,
            w.at[slot],
            ring_send.at[FIRST[i] + k],
            ring_recv.at[FIRST[i] + k],
            s,
            dp_of(direction),
        )

    def gathered(i, k):
        direction, bit, _ = CHAINS[i]
        slot = z_of(-direction * (k + 1)) * 4 + flipped(bit) * 2 + core
        return slot, remote(
            w.at[slot],
            w.at[slot],
            ring_send.at[FIRST[i] + k],
            ring_recv.at[FIRST[i] + k],
            s,
            dp_of(direction),
        )

    def to_sibling(slot, index, src=None):
        return remote(
            w.at[slot] if src is None else src,
            w.at[slot],
            sib_send.at[index],
            sib_recv.at[index],
            s,
            sibling,
        )

    def from_sibling(slot, index):
        other = slot + 1 - 2 * core
        return remote(w.at[other], w.at[other], sib_send.at[index], sib_recv.at[index], s, sibling)

    exchange = remote(shard, w.at[d], y_send.at[0], y_recv.at[0], s, other_y)
    exchange.start()
    sends = [exchange, gather_copy(0, 0, shard), gather_copy(3, 0, shard), to_sibling(d, 14, shard)]
    for copy in sends[1:]:
        copy.start()

    grad_copy = remote(grad, up, sec_send.at[0], sec_recv.at[0], before, d)
    grad_copy.start()

    load_slots.wait()
    mine_fetch = plan[s, 0]
    mine_keep = plan[s, 1]
    theirs_fetch = plan[partner, 0]
    theirs_keep = plan[partner, 1]

    def pick(c, carry):
        at = pl.ds(pl.multiple_of(c * CHIP, 128), CHIP)
        first = slots[0, :, at].astype(F32)
        second = slots[1, :, at].astype(F32)
        wanted[:, at] = jnp.where(theirs_fetch >= 3, second, first).astype(BF16)
        return carry

    lax.fori_loop(0, chips, pick, 0)
    wanted_copy = remote(wanted, stash, sec_send.at[1], sec_recv.at[1], partner, d)
    wanted_copy.start()

    slot_y = z * 4 + (1 - y) * 2 + core
    remote(w.at[slot_y], w.at[slot_y], y_send.at[0], y_recv.at[0], s, other_y).wait_recv()
    more = [gather_copy(1, 0), gather_copy(2, 0), to_sibling(slot_y, 15)]
    for copy in more:
        copy.start()
    sends += more
    sib_slots = [(d, 14), (slot_y, 15)]
    for k in range(4):
        for i, (_, _, hops) in enumerate(CHAINS):
            if k >= hops:
                continue
            slot, arrival = gathered(i, k)
            arrival.wait_recv()
            if k + 1 < hops:
                copy = gather_copy(i, k + 1)
                copy.start()
                sends.append(copy)
            copy = to_sibling(slot, FIRST[i] + k)
            copy.start()
            sends.append(copy)
            sib_slots.append((slot, FIRST[i] + k))
    for slot, index in sib_slots:
        from_sibling(slot, index).wait_recv()
    keep_shard.wait()

    def w_in_of(c):
        return jnp.concatenate([w[2 * c, :HALF, :], w[2 * c + 1, :HALF, :]], axis=0)

    def w_out_of(c):
        return jnp.concatenate([w[2 * c, HALF:CHIP, :], w[2 * c + 1, HALF:CHIP, :]], axis=0)

    def gain_of(c):
        both = w[2 * c, CHIP:PACK, :].astype(F32) + w[2 * c + 1, CHIP:PACK, :].astype(F32)
        return both[:1]

    def lanes(c):
        return pl.ds(pl.multiple_of(c * CHIP, 128), CHIP)

    def folded(v):
        return v[:, :128] + v[:, 128:256] + v[:, 256:]

    def stats(ref):
        zero = jnp.zeros((rows, 128), F32)
        total = lax.fori_loop(
            0, chips, lambda c, acc: acc + folded(ref[:, lanes(c)].astype(F32)), zero
        )
        mean = jnp.sum(total, axis=1, keepdims=True) / width

        def spread(c, acc):
            centred = ref[:, lanes(c)].astype(F32) - mean
            return acc + folded(centred * centred)

        total = lax.fori_loop(0, chips, spread, zero)
        inverse = lax.rsqrt(jnp.sum(total, axis=1, keepdims=True) / width + EPSILON)
        return mean, inverse

    wanted_copy.wait_recv()

    def choose(c, carry):
        at = lanes(c)
        own = jnp.where(mine_fetch >= 1, slots[1, :, at].astype(F32), slots[0, :, at].astype(F32))
        stash[:, at] = jnp.where(mine_fetch >= 2, stash[:, at].astype(F32), own).astype(BF16)
        return carry

    lax.fori_loop(0, chips, choose, 0)
    mean_z, inverse_z = stats(stash)
    grad_copy.wait_recv()

    act_copy = remote(act, xin, sec_send.at[2], sec_recv.at[2], after, d)
    act_copy.start()
    pin_copy = remote(act, pin, sec_send.at[3], sec_recv.at[3], across, d)
    pin_local = pltpu.make_async_copy(act, pin, local.at[2])

    @pl.when(across != s)
    def _():
        pin_copy.start()

    @pl.when(across == s)
    def _():
        pin_local.start()

    def pre_step(c, carry):
        pre, d_hidden = carry
        at = lanes(c)
        unit = (stash[:, at].astype(F32) - mean_z) * inverse_z
        rounded = (unit * gain_of(c)).astype(BF16)
        normed[:, at] = rounded
        pre += jnp.dot(rounded, w_in_of(c), preferred_element_type=F32)
        d_hidden += jnp.dot(up[:, at], w_out_of(c), preferred_element_type=F32)
        return pre, d_hidden

    zero = jnp.zeros((rows, CHIP), F32)
    pre, d_hidden = lax.fori_loop(0, chips, pre_step, (zero, zero))
    hidden, slope = gelu_and_slope(pre)
    hidden = hidden.astype(BF16)
    d_pre = (d_hidden * slope).astype(BF16)

    def half_copy(chip):
        return remote(
            part.at[chip, 1 - core],
            sib_part.at[chip],
            half_send.at[chip],
            half_recv.at[chip],
            s,
            sibling,
        )

    def chip_at(i, k):
        direction, bit, hops = CHAINS[i]
        return z_of(direction * (hops - k)) * 2 + flipped(bit)

    order = [chip_at(i, k) for k in range(4) for i in range(4) if k < CHAINS[i][2]]
    own_far = z * 2 + flipped(1)
    own_near = z * 2 + y
    order += [own_far, own_near]

    def partials(chip, row_sums):
        at = lanes(chip)
        rounded = normed[:, at]
        u = up[:, at]
        p_in = lax.dot_general(rounded, d_pre, ROWS_IN_COMMON, preferred_element_type=F32)
        p_out = lax.dot_general(u, hidden, ROWS_IN_COMMON, preferred_element_type=F32)
        p_in = p_in.astype(BF16)
        p_out = p_out.astype(BF16)
        d_normed = lax.dot_general(d_pre, w_in_of(chip), COLS_IN_COMMON, preferred_element_type=F32)
        unit = (stash[:, at].astype(F32) - mean_z) * inverse_z
        p_gain = jnp.sum(d_normed * unit, axis=0, keepdims=True)
        p_gain = jnp.broadcast_to(p_gain, (16, CHIP)).astype(BF16)
        for half in range(2):
            part[chip, half, :HALF, :] = p_in[half * HALF : (half + 1) * HALF]
            part[chip, half, HALF:CHIP, :] = p_out[half * HALF : (half + 1) * HALF]
            part[chip, half, CHIP:PACK, :] = p_gain
        half_copy(chip).start()
        d_u = d_normed * gain_of(chip)
        d_unit[:, at] = d_u
        return row_sums[0] + folded(d_u), row_sums[1] + folded(d_u * unit)

    row_sums = (jnp.zeros((rows, 128), F32), jnp.zeros((rows, 128), F32))

    def chain_copy(i, k):
        return remote(
            part.at[chip_at(i, k), core],
            chain_in.at[FIRST[i] + k],
            chain_send.at[FIRST[i] + k],
            chain_recv.at[FIRST[i] + k],
            s,
            dp_of(CHAINS[i][0]),
        )

    def chip_sum(chip, *arrived):
        half_copy(chip).wait_recv()
        total = part[chip, core].astype(F32) + sib_part[chip].astype(F32)
        for index in arrived:
            total += chain_in[index].astype(F32)
        return total

    def chain_step(i, k):
        chip = chip_at(i, k)
        arrived = ()
        if k > 0:
            chain_copy(i, k - 1).wait_recv()
            arrived = (FIRST[i] + k - 1,)
        part[chip, core] = chip_sum(chip, *arrived).astype(BF16)
        chain_copy(i, k).start()

    entries = [(i, k) for k in range(4) for i in range(4) if k < CHAINS[i][2]]
    for chip in order:
        row_sums = partials(chip, row_sums)
    for i, k in entries:
        chain_step(i, k)

    mean_d = jnp.sum(row_sums[0], axis=1, keepdims=True) / width
    mean_du = jnp.sum(row_sums[1], axis=1, keepdims=True) / width

    def input_grad(c, carry):
        at = lanes(c)
        unit = (stash[:, at].astype(F32) - mean_z) * inverse_z
        change = inverse_z * (d_unit[:, at] - mean_d - unit * mean_du)
        normed[:, at] = (up[:, at].astype(F32) + change).astype(BF16)
        return carry

    lax.fori_loop(0, chips, input_grad, 0)
    store_grad = pltpu.make_async_copy(normed, grad_next, local.at[3])
    store_grad.start()

    for i in (1, 2):
        chain_copy(i, CHAINS[i][2] - 1).wait_recv()
    part[own_far, core] = chip_sum(
        own_far, FIRST[1] + CHAINS[1][2] - 1, FIRST[2] + CHAINS[2][2] - 1
    ).astype(BF16)
    last_copy = remote(
        part.at[own_far, core], last_in, last_send.at[0], last_recv.at[0], s, other_y
    )
    last_copy.start()

    act_copy.wait_recv()
    mean_x, inverse_x = stats(xin)

    def pre_x_step(c, pre_x):
        unit = (xin[:, lanes(c)].astype(F32) - mean_x) * inverse_x
        rounded = (unit * gain_of(c)).astype(BF16)
        return pre_x + jnp.dot(rounded, w_in_of(c), preferred_element_type=F32)

    hidden_x, _ = gelu_and_slope(lax.fori_loop(0, chips, pre_x_step, zero))
    hidden_x = hidden_x.astype(BF16)

    def forward_step(c, carry):
        at = lanes(c)
        added = lax.dot_general(hidden_x, w_out_of(c), COLS_IN_COMMON, preferred_element_type=F32)
        out_act[:, at] = (xin[:, at].astype(F32) + added).astype(BF16)
        return carry

    lax.fori_loop(0, chips, forward_step, 0)
    store_act = pltpu.make_async_copy(out_act, act_next, local.at[4])
    store_act.start()

    @pl.when(across != s)
    def _():
        pin_copy.wait()

    @pl.when(across == s)
    def _():
        pin_local.wait()

    def keep(c, carry):
        at = lanes(c)
        for j in range(2):
            value = jnp.where(
                theirs_keep == j + 2, pin[:, at].astype(F32), slots[j, :, at].astype(F32)
            )
            slots[j, :, at] = jnp.where(mine_keep == j, xin[:, at].astype(F32), value).astype(BF16)
        return carry

    lax.fori_loop(0, chips, keep, 0)
    store_pool = pltpu.make_async_copy(slots, pool_next, local.at[5])
    store_pool.start()

    for i in (0, 3):
        chain_copy(i, CHAINS[i][2] - 1).wait_recv()
    total = chip_sum(own_near, FIRST[0] + CHAINS[0][2] - 1, FIRST[3] + CHAINS[3][2] - 1)
    last_copy.wait_recv()
    sums[...] = total + last_in[...].astype(F32)

    for copy in sends:
        copy.wait_send()
    grad_copy.wait_send()
    wanted_copy.wait_send()
    act_copy.wait_send()
    for chip in order:
        half_copy(chip).wait_send()
    for i, k in entries:
        chain_copy(i, k).wait_send()
    last_copy.wait_send()
    store_grad.wait()
    store_act.wait()
    store_pool.wait()


def per_device(act_sent, grad_sent, stash_pool, w_in, w_out, gain, plan):
    rows, width = act_sent.shape[1:]
    core = lax.axis_index("dp") % 2
    gain_row = jnp.tile(gain, (1, 2))
    lane = lax.broadcasted_iota(jnp.int32, gain_row.shape, 1)
    gain_row = jnp.where(lane // HALF == core, gain_row, jnp.zeros_like(gain_row))
    shard = jnp.concatenate(
        [w_in[0], w_out[0].T, jnp.broadcast_to(gain_row, (16, CHIP))], axis=0
    )
    anywhere = pl.BlockSpec(memory_space=pl.ANY)
    vmem = pl.BlockSpec(memory_space=pltpu.VMEM)
    block = jax.ShapeDtypeStruct((rows, width), BF16)
    chips = width // CHIP
    dma = pltpu.SemaphoreType.DMA
    act_next, grad_next, pool_next, sums = pl.pallas_call(
        tick_kernel,
        out_shape=(
            block,
            block,
            jax.ShapeDtypeStruct((2, rows, width), BF16),
            jax.ShapeDtypeStruct((PACK, CHIP), F32),
        ),
        in_specs=[
            vmem,
            pl.BlockSpec(memory_space=pltpu.SMEM),
            anywhere,
            anywhere,
            anywhere,
        ],
        out_specs=(anywhere, anywhere, anywhere, vmem),
        scratch_shapes=[
            pltpu.VMEM((2 * chips, PACK, CHIP), BF16),
            pltpu.VMEM((chips, 2, PACK, CHIP), BF16),
            pltpu.VMEM((chips, PACK, CHIP), BF16),
            pltpu.VMEM((STEPS, PACK, CHIP), BF16),
            pltpu.VMEM((PACK, CHIP), BF16),
            pltpu.VMEM((2, rows, width), BF16),
            pltpu.VMEM((rows, width), BF16),
            pltpu.VMEM((rows, width), BF16),
            pltpu.VMEM((rows, width), BF16),
            pltpu.VMEM((rows, width), BF16),
            pltpu.VMEM((rows, width), BF16),
            pltpu.VMEM((rows, width), BF16),
            pltpu.VMEM((rows, width), F32),
            pltpu.VMEM((rows, width), BF16),
            dma((STEPS,)),
            dma((STEPS,)),
            dma((16,)),
            dma((16,)),
            dma((1,)),
            dma((1,)),
            dma((4,)),
            dma((4,)),
            dma((STEPS,)),
            dma((STEPS,)),
            dma((chips,)),
            dma((chips,)),
            dma((1,)),
            dma((1,)),
            dma((6,)),
        ],
        compiler_params=pltpu.CompilerParams(
            collective_id=0, has_side_effects=True, vmem_limit_bytes=60 * 1024 * 1024
        ),
        cost_estimate=pl.CostEstimate(
            flops=14 * rows * width * CHIP, bytes_accessed=20 * rows * width, transcendentals=0
        ),
    )(shard, plan, act_sent[0], grad_sent[0], stash_pool[0])
    sum_gain = lax.dynamic_slice_in_dim(sums[CHIP], core * HALF, HALF)
    return (
        act_next[None],
        grad_next[None],
        pool_next[None],
        sums[None, :HALF],
        sums[HALF:CHIP].T[None],
        sum_gain[None],
    )


def solution(mesh):
    placed = (
        P("section", "dp", None),
        P("section", "dp", None),
        P("section", None, "dp", None),
        P("section", "dp", None),
        P("section", None, "dp"),
        P("section", "dp"),
        P(),
    )
    return jax.shard_map(
        per_device,
        mesh=mesh,
        in_specs=placed,
        out_specs=(
            P("section", "dp", None),
            P("section", "dp", None),
            P("section", None, "dp", None),
            P("section", "dp", None),
            P("section", None, "dp"),
            P("section", "dp"),
        ),
        check_vma=False,
    )
```

```python
import jax
import jax.numpy as jnp
from jax import lax
from jax.experimental import pallas as pl
from jax.experimental.pallas import tpu as pltpu
from jax.sharding import PartitionSpec as P

EPSILON = 1e-05
MESH = pl.DeviceIdType.MESH
F32 = jnp.float32
BF16 = jnp.bfloat16
ROWS_IN_COMMON = (((0,), (0,)), ((), ()))
COLS_IN_COMMON = (((1,), (1,)), ((), ()))

NZ = 8
HALF = 192
CHIP = 2 * HALF
PACK = 2 * HALF + 16

CHAINS = ((1, 0, 4), (-1, 1, 4), (1, 1, 3), (-1, 0, 3))
FIRST = (0, 4, 8, 11)
STEPS = 14
SLICES = 8
PIECES = 4


def remote(src, dst, send_sem, recv_sem, section, dp):
    return pltpu.make_async_remote_copy(
        src_ref=src,
        dst_ref=dst,
        send_sem=send_sem,
        recv_sem=recv_sem,
        device_id=(section, dp),
        device_id_type=MESH,
    )


def gelu_and_slope(x):
    c = 0.7978845608028654
    a = 0.044715
    t = jnp.tanh(c * (x + a * (x * x * x)))
    hidden = x * (0.5 * (1.0 + t))
    slope = 0.5 * (1.0 + t) + 0.5 * x * (1.0 - t * t) * (c * (1.0 + 3.0 * a * (x * x)))
    return hidden, slope


def tick_kernel(
    shard,
    plan,
    act,
    grad,
    pool,
    act_next,
    grad_next,
    pool_next,
    sums,
    w,
    part,
    sib_part,
    chain_in,
    last_in,
    slots,
    wanted,
    stash,
    up,
    xin,
    pin,
    normed,
    d_unit,
    out_act,
    ring_send,
    ring_recv,
    sib_send,
    sib_recv,
    y_send,
    y_recv,
    grad_send,
    grad_recv,
    wanted_send,
    wanted_recv,
    act_send,
    act_recv,
    pin_send,
    pin_recv,
    chain_send,
    chain_recv,
    half_send,
    half_recv,
    last_send,
    last_recv,
    local,
):
    rows, width = act.shape
    chips = width // CHIP
    s = lax.axis_index("section")
    d = lax.axis_index("dp")
    core = d % 2
    y = (d // 2) % 2
    z = d // 4
    sections = lax.axis_size("section")
    after = (s + 1) % sections
    before = (s + sections - 1) % sections
    partner = sections - 1 - s
    across = (2 * sections - 2 - s) % sections
    sibling = z * 4 + y * 2 + (1 - core)
    other_y = z * 4 + (1 - y) * 2 + core

    def z_of(step):
        return (z + step + 2 * NZ) % NZ

    def dp_of(step):
        return z_of(step) * 4 + y * 2 + core

    def flipped(bit):
        return (y + bit) % 2

    load_slots = pltpu.make_async_copy(pool, slots, local.at[0])
    load_slots.start()
    keep_shard = pltpu.make_async_copy(shard, w.at[d], local.at[1])
    keep_shard.start()

    barrier = pltpu.get_barrier_semaphore()
    for target in (
        (s, sibling),
        (s, other_y),
        (s, dp_of(1)),
        (s, dp_of(-1)),
        (after, d),
        (before, d),
        (partner, d),
    ):
        pl.semaphore_signal(barrier, inc=1, device_id=target, device_id_type=MESH)

    @pl.when(across != s)
    def _():
        pl.semaphore_signal(barrier, inc=1, device_id=(across, d), device_id_type=MESH)
        pl.semaphore_wait(barrier, 8)

    @pl.when(across == s)
    def _():
        pl.semaphore_wait(barrier, 7)

    def gather_copy(i, k, src=None):
        direction, bit, _ = CHAINS[i]
        slot = z_of(-direction * k) * 4 + flipped(bit) * 2 + core
        return remote(
            w.at[slot] if src is None else src,
            w.at[slot],
            ring_send.at[FIRST[i] + k],
            ring_recv.at[FIRST[i] + k],
            s,
            dp_of(direction),
        )

    def gathered(i, k):
        direction, bit, _ = CHAINS[i]
        slot = z_of(-direction * (k + 1)) * 4 + flipped(bit) * 2 + core
        return slot, remote(
            w.at[slot],
            w.at[slot],
            ring_send.at[FIRST[i] + k],
            ring_recv.at[FIRST[i] + k],
            s,
            dp_of(direction),
        )

    def to_sibling(slot, index, src=None):
        return remote(
            w.at[slot] if src is None else src,
            w.at[slot],
            sib_send.at[index],
            sib_recv.at[index],
            s,
            sibling,
        )

    def from_sibling(slot, index):
        other = slot + 1 - 2 * core
        return remote(w.at[other], w.at[other], sib_send.at[index], sib_recv.at[index], s, sibling)

    exchange = remote(shard, w.at[d], y_send.at[0], y_recv.at[0], s, other_y)
    exchange.start()
    sends = [exchange, gather_copy(0, 0, shard), gather_copy(3, 0, shard), to_sibling(d, 14, shard)]
    for copy in sends[1:]:
        copy.start()

    load_slots.wait()
    mine_fetch = plan[s, 0]
    mine_keep = plan[s, 1]
    theirs_fetch = plan[partner, 0]
    theirs_keep = plan[partner, 1]

    def pick(c, carry):
        at = pl.ds(pl.multiple_of(c * CHIP, 128), CHIP)
        first = slots[0, :, at].astype(F32)
        second = slots[1, :, at].astype(F32)
        wanted[:, at] = jnp.where(theirs_fetch >= 3, second, first).astype(BF16)
        return carry

    lax.fori_loop(0, chips, pick, 0)

    def wanted_copy(n):
        at = pl.ds(n * (rows // PIECES), rows // PIECES)
        return remote(wanted.at[at], stash.at[at], wanted_send.at[n], wanted_recv.at[n], partner, d)


    slot_y = z * 4 + (1 - y) * 2 + core
    remote(w.at[slot_y], w.at[slot_y], y_send.at[0], y_recv.at[0], s, other_y).wait_recv()
    for n in range(PIECES):
        wanted_copy(n).start()
    more = [gather_copy(1, 0), gather_copy(2, 0), to_sibling(slot_y, 15)]
    for copy in more:
        copy.start()
    sends += more
    sib_slots = [(d, 14), (slot_y, 15)]
    def gather_round(k):
        for i, (_, _, hops) in enumerate(CHAINS):
            if k >= hops:
                continue
            slot, arrival = gathered(i, k)
            arrival.wait_recv()
            if k + 1 < hops:
                copy = gather_copy(i, k + 1)
                copy.start()
                sends.append(copy)
            copy = to_sibling(slot, FIRST[i] + k)
            copy.start()
            sends.append(copy)
            sib_slots.append((slot, FIRST[i] + k))

    piece = width // PIECES

    def grad_copy(n):
        at = pl.ds(n * piece, piece)
        return remote(grad.at[:, at], up.at[:, at], grad_send.at[n], grad_recv.at[n], before, d)

    def act_copy(n):
        at = pl.ds(n * (rows // SLICES), rows // SLICES)
        return remote(act.at[at], xin.at[at], act_send.at[n], act_recv.at[n], after, d)

    def pin_copy(n):
        at = pl.ds(n * (rows // SLICES), rows // SLICES)
        return remote(act.at[at], pin.at[at], pin_send.at[n], pin_recv.at[n], across, d)

    pin_local = pltpu.make_async_copy(act, pin, local.at[2])

    gather_round(0)
    gather_round(1)
    for n in range(PIECES - 1):
        wanted_copy(n).wait_recv()
    for n in range(PIECES):
        grad_copy(n).start()

    @pl.when(across == s)
    def _():
        pin_local.start()

    gather_round(2)

    def w_in_of(c):
        return jnp.concatenate([w[2 * c, :HALF, :], w[2 * c + 1, :HALF, :]], axis=0)

    def w_out_of(c):
        return jnp.concatenate([w[2 * c, HALF:CHIP, :], w[2 * c + 1, HALF:CHIP, :]], axis=0)

    def gain_of(c):
        both = w[2 * c, CHIP:PACK, :].astype(F32) + w[2 * c + 1, CHIP:PACK, :].astype(F32)
        return both[:1]

    def lanes(c):
        return pl.ds(pl.multiple_of(c * CHIP, 128), CHIP)

    def folded(v):
        return v[:, :128] + v[:, 128:256] + v[:, 256:]

    def stats(ref):
        zero = jnp.zeros((rows, 128), F32)
        total = lax.fori_loop(
            0, chips, lambda c, acc: acc + folded(ref[:, lanes(c)].astype(F32)), zero
        )
        mean = jnp.sum(total, axis=1, keepdims=True) / width

        def spread(c, acc):
            centred = ref[:, lanes(c)].astype(F32) - mean
            return acc + folded(centred * centred)

        total = lax.fori_loop(0, chips, spread, zero)
        inverse = lax.rsqrt(jnp.sum(total, axis=1, keepdims=True) / width + EPSILON)
        return mean, inverse

    wanted_copy(PIECES - 1).wait_recv()

    def choose(c, carry):
        at = lanes(c)
        own = jnp.where(mine_fetch >= 1, slots[1, :, at].astype(F32), slots[0, :, at].astype(F32))
        stash[:, at] = jnp.where(mine_fetch >= 2, stash[:, at].astype(F32), own).astype(BF16)
        return carry

    lax.fori_loop(0, chips, choose, 0)
    mean_z, inverse_z = stats(stash)
    gather_round(3)
    for slot, index in sib_slots:
        from_sibling(slot, index).wait_recv()
    keep_shard.wait()

    def pre_step(c, pre):
        at = lanes(c)
        unit = (stash[:, at].astype(F32) - mean_z) * inverse_z
        rounded = (unit * gain_of(c)).astype(BF16)
        normed[:, at] = rounded
        return pre + jnp.dot(rounded, w_in_of(c), preferred_element_type=F32)

    def d_hidden_step(c, d_hidden):
        return d_hidden + jnp.dot(up[:, lanes(c)], w_out_of(c), preferred_element_type=F32)

    zero = jnp.zeros((rows, CHIP), F32)
    hidden, slope = gelu_and_slope(lax.fori_loop(0, chips, pre_step, zero))
    hidden = hidden.astype(BF16)
    d_hidden = zero
    for n in range(PIECES):
        grad_copy(n).wait_recv()
        first = n * (chips // PIECES)
        d_hidden = lax.fori_loop(first, first + chips // PIECES, d_hidden_step, d_hidden)
    d_pre = (d_hidden * slope).astype(BF16)

    def half_copy(chip):
        return remote(
            part.at[chip, 1 - core],
            sib_part.at[chip],
            half_send.at[chip],
            half_recv.at[chip],
            s,
            sibling,
        )

    def chip_at(i, k):
        direction, bit, hops = CHAINS[i]
        return z_of(direction * (hops - k)) * 2 + flipped(bit)

    entries = [(i, k) for k in range(4) for i in (1, 2, 0, 3) if k < CHAINS[i][2]]
    order = [chip_at(i, k) for i, k in entries]
    own_far = z * 2 + flipped(1)
    own_near = z * 2 + y
    order += [own_far, own_near]

    def partials(chip, row_sums):
        at = lanes(chip)
        rounded = normed[:, at]
        u = up[:, at]
        p_in = lax.dot_general(rounded, d_pre, ROWS_IN_COMMON, preferred_element_type=F32)
        p_out = lax.dot_general(u, hidden, ROWS_IN_COMMON, preferred_element_type=F32)
        p_in = p_in.astype(BF16)
        p_out = p_out.astype(BF16)
        d_normed = lax.dot_general(d_pre, w_in_of(chip), COLS_IN_COMMON, preferred_element_type=F32)
        unit = (stash[:, at].astype(F32) - mean_z) * inverse_z
        p_gain = jnp.sum(d_normed * unit, axis=0, keepdims=True)
        p_gain = jnp.broadcast_to(p_gain, (16, CHIP)).astype(BF16)
        for half in range(2):
            part[chip, half, :HALF, :] = p_in[half * HALF : (half + 1) * HALF]
            part[chip, half, HALF:CHIP, :] = p_out[half * HALF : (half + 1) * HALF]
            part[chip, half, CHIP:PACK, :] = p_gain
        half_copy(chip).start()
        d_u = d_normed * gain_of(chip)
        d_unit[:, at] = d_u
        return row_sums[0] + folded(d_u), row_sums[1] + folded(d_u * unit)

    row_sums = (jnp.zeros((rows, 128), F32), jnp.zeros((rows, 128), F32))

    def chain_copy(i, k):
        return remote(
            part.at[chip_at(i, k), core],
            chain_in.at[FIRST[i] + k],
            chain_send.at[FIRST[i] + k],
            chain_recv.at[FIRST[i] + k],
            s,
            dp_of(CHAINS[i][0]),
        )

    def chip_sum(chip, *arrived):
        half_copy(chip).wait_recv()
        total = part[chip, core].astype(F32) + sib_part[chip].astype(F32)
        for index in arrived:
            total += chain_in[index].astype(F32)
        return total

    def chain_step(i, k):
        chip = chip_at(i, k)
        arrived = ()
        if k > 0:
            chain_copy(i, k - 1).wait_recv()
            arrived = (FIRST[i] + k - 1,)
        part[chip, core] = chip_sum(chip, *arrived).astype(BF16)
        chain_copy(i, k).start()
        n = entries.index((i, k))
        if 2 <= n < 2 + SLICES:
            act_copy(n - 2).start()
        if 4 <= n < 4 + SLICES:

            @pl.when(across != s)
            def _():
                pin_copy(n - 4).start()

    for n, chip in enumerate(order):
        row_sums = partials(chip, row_sums)
        if 1 <= n <= 4:
            chain_step(*entries[n - 1])
    for i, k in entries[4:8]:
        chain_step(i, k)

    mean_d = jnp.sum(row_sums[0], axis=1, keepdims=True) / width
    mean_du = jnp.sum(row_sums[1], axis=1, keepdims=True) / width

    def input_grad(c, carry):
        at = lanes(c)
        unit = (stash[:, at].astype(F32) - mean_z) * inverse_z
        change = inverse_z * (d_unit[:, at] - mean_d - unit * mean_du)
        normed[:, at] = (up[:, at].astype(F32) + change).astype(BF16)
        return carry

    lax.fori_loop(0, chips, input_grad, 0)
    store_grad = pltpu.make_async_copy(normed, grad_next, local.at[3])
    store_grad.start()
    for i, k in entries[8:]:
        chain_step(i, k)

    for i in (1, 2):
        chain_copy(i, CHAINS[i][2] - 1).wait_recv()
    part[own_far, core] = chip_sum(
        own_far, FIRST[1] + CHAINS[1][2] - 1, FIRST[2] + CHAINS[2][2] - 1
    ).astype(BF16)
    last_copy = remote(
        part.at[own_far, core], last_in, last_send.at[0], last_recv.at[0], s, other_y
    )
    last_copy.start()

    for n in range(SLICES):
        act_copy(n).wait_recv()
    mean_x, inverse_x = stats(xin)

    def pre_x_step(c, pre_x):
        unit = (xin[:, lanes(c)].astype(F32) - mean_x) * inverse_x
        rounded = (unit * gain_of(c)).astype(BF16)
        return pre_x + jnp.dot(rounded, w_in_of(c), preferred_element_type=F32)

    hidden_x, _ = gelu_and_slope(lax.fori_loop(0, chips, pre_x_step, zero))
    hidden_x = hidden_x.astype(BF16)

    def forward_step(c, carry):
        at = lanes(c)
        added = lax.dot_general(hidden_x, w_out_of(c), COLS_IN_COMMON, preferred_element_type=F32)
        out_act[:, at] = (xin[:, at].astype(F32) + added).astype(BF16)
        return carry

    lax.fori_loop(0, chips, forward_step, 0)
    store_act = pltpu.make_async_copy(out_act, act_next, local.at[4])
    store_act.start()

    @pl.when(across != s)
    def _():
        for n in range(SLICES):
            pin_copy(n).wait()

    @pl.when(across == s)
    def _():
        pin_local.wait()

    def keep(c, carry):
        at = lanes(c)
        for j in range(2):
            value = jnp.where(
                theirs_keep == j + 2, pin[:, at].astype(F32), slots[j, :, at].astype(F32)
            )
            slots[j, :, at] = jnp.where(mine_keep == j, xin[:, at].astype(F32), value).astype(BF16)
        return carry

    lax.fori_loop(0, chips, keep, 0)
    store_pool = pltpu.make_async_copy(slots, pool_next, local.at[5])
    store_pool.start()

    for i in (0, 3):
        chain_copy(i, CHAINS[i][2] - 1).wait_recv()
    total = chip_sum(own_near, FIRST[0] + CHAINS[0][2] - 1, FIRST[3] + CHAINS[3][2] - 1)
    last_copy.wait_recv()
    sums[...] = total + last_in[...].astype(F32)

    for copy in sends:
        copy.wait_send()
    for n in range(PIECES):
        grad_copy(n).wait_send()
        wanted_copy(n).wait_send()
    for n in range(SLICES):
        act_copy(n).wait_send()
    for chip in order:
        half_copy(chip).wait_send()
    for i, k in entries:
        chain_copy(i, k).wait_send()
    last_copy.wait_send()
    store_grad.wait()
    store_act.wait()
    store_pool.wait()


def per_device(act_sent, grad_sent, stash_pool, w_in, w_out, gain, plan):
    rows, width = act_sent.shape[1:]
    core = lax.axis_index("dp") % 2
    gain_row = jnp.tile(gain, (1, 2))
    lane = lax.broadcasted_iota(jnp.int32, gain_row.shape, 1)
    gain_row = jnp.where(lane // HALF == core, gain_row, jnp.zeros_like(gain_row))
    shard = jnp.concatenate(
        [w_in[0], w_out[0].T, jnp.broadcast_to(gain_row, (16, CHIP))], axis=0
    )
    anywhere = pl.BlockSpec(memory_space=pl.ANY)
    vmem = pl.BlockSpec(memory_space=pltpu.VMEM)
    block = jax.ShapeDtypeStruct((rows, width), BF16)
    chips = width // CHIP
    dma = pltpu.SemaphoreType.DMA
    act_next, grad_next, pool_next, sums = pl.pallas_call(
        tick_kernel,
        out_shape=(
            block,
            block,
            jax.ShapeDtypeStruct((2, rows, width), BF16),
            jax.ShapeDtypeStruct((PACK, CHIP), F32),
        ),
        in_specs=[
            vmem,
            pl.BlockSpec(memory_space=pltpu.SMEM),
            anywhere,
            anywhere,
            anywhere,
        ],
        out_specs=(anywhere, anywhere, anywhere, vmem),
        scratch_shapes=[
            pltpu.VMEM((2 * chips, PACK, CHIP), BF16),
            pltpu.VMEM((chips, 2, PACK, CHIP), BF16),
            pltpu.VMEM((chips, PACK, CHIP), BF16),
            pltpu.VMEM((STEPS, PACK, CHIP), BF16),
            pltpu.VMEM((PACK, CHIP), BF16),
            pltpu.VMEM((2, rows, width), BF16),
            pltpu.VMEM((rows, width), BF16),
            pltpu.VMEM((rows, width), BF16),
            pltpu.VMEM((rows, width), BF16),
            pltpu.VMEM((rows, width), BF16),
            pltpu.VMEM((rows, width), BF16),
            pltpu.VMEM((rows, width), BF16),
            pltpu.VMEM((rows, width), F32),
            pltpu.VMEM((rows, width), BF16),
            dma((STEPS,)),
            dma((STEPS,)),
            dma((16,)),
            dma((16,)),
            dma((1,)),
            dma((1,)),
            dma((PIECES,)),
            dma((PIECES,)),
            dma((PIECES,)),
            dma((PIECES,)),
            dma((SLICES,)),
            dma((SLICES,)),
            dma((SLICES,)),
            dma((SLICES,)),
            dma((STEPS,)),
            dma((STEPS,)),
            dma((chips,)),
            dma((chips,)),
            dma((1,)),
            dma((1,)),
            dma((6,)),
        ],
        compiler_params=pltpu.CompilerParams(
            collective_id=0, has_side_effects=True, vmem_limit_bytes=60 * 1024 * 1024
        ),
        cost_estimate=pl.CostEstimate(
            flops=14 * rows * width * CHIP, bytes_accessed=20 * rows * width, transcendentals=0
        ),
    )(shard, plan, act_sent[0], grad_sent[0], stash_pool[0])
    sum_gain = lax.dynamic_slice_in_dim(sums[CHIP], core * HALF, HALF)
    return (
        act_next[None],
        grad_next[None],
        pool_next[None],
        sums[None, :HALF],
        sums[HALF:CHIP].T[None],
        sum_gain[None],
    )


def solution(mesh):
    placed = (
        P("section", "dp", None),
        P("section", "dp", None),
        P("section", None, "dp", None),
        P("section", "dp", None),
        P("section", None, "dp"),
        P("section", "dp"),
        P(),
    )
    return jax.shard_map(
        per_device,
        mesh=mesh,
        in_specs=placed,
        out_specs=(
            P("section", "dp", None),
            P("section", "dp", None),
            P("section", None, "dp", None),
            P("section", "dp", None),
            P("section", None, "dp"),
            P("section", "dp"),
        ),
        check_vma=False,
    )
```

```python
import jax
import jax.numpy as jnp
from jax import lax
from jax.experimental import pallas as pl
from jax.experimental.pallas import tpu as pltpu
from jax.sharding import PartitionSpec as P

EPSILON = 1e-05
MESH = pl.DeviceIdType.MESH
F32 = jnp.float32
BF16 = jnp.bfloat16
ROWS_IN_COMMON = (((0,), (0,)), ((), ()))
COLS_IN_COMMON = (((1,), (1,)), ((), ()))

NZ = 8
HALF = 192
CHIP = 2 * HALF
PACK = 2 * HALF + 16

CHAINS = ((1, 0, 4), (-1, 1, 4), (1, 1, 3), (-1, 0, 3))
FIRST = (0, 4, 8, 11)
STEPS = 14
ACT_STEPS = (4, 5, 6, 7)
SLICES = 8
PIECES = 4


def remote(src, dst, send_sem, recv_sem, section, dp):
    return pltpu.make_async_remote_copy(
        src_ref=src,
        dst_ref=dst,
        send_sem=send_sem,
        recv_sem=recv_sem,
        device_id=(section, dp),
        device_id_type=MESH,
    )


def gelu_and_slope(x):
    c = 0.7978845608028654
    a = 0.044715
    t = jnp.tanh(c * (x + a * (x * x * x)))
    hidden = x * (0.5 * (1.0 + t))
    slope = 0.5 * (1.0 + t) + 0.5 * x * (1.0 - t * t) * (c * (1.0 + 3.0 * a * (x * x)))
    return hidden, slope


def tick_kernel(
    shard,
    plan,
    act,
    grad,
    pool,
    act_next,
    grad_next,
    pool_next,
    sums,
    w,
    part,
    sib_part,
    chain_in,
    last_in,
    slots,
    wanted,
    stash,
    up,
    xin,
    pin,
    normed,
    d_unit,
    out_act,
    ring_send,
    ring_recv,
    sib_send,
    sib_recv,
    y_send,
    y_recv,
    grad_send,
    grad_recv,
    wanted_send,
    wanted_recv,
    act_send,
    act_recv,
    pin_send,
    pin_recv,
    chain_send,
    chain_recv,
    half_send,
    half_recv,
    last_send,
    last_recv,
    local,
):
    rows, width = act.shape
    chips = width // CHIP
    s = lax.axis_index("section")
    d = lax.axis_index("dp")
    core = d % 2
    y = (d // 2) % 2
    z = d // 4
    sections = lax.axis_size("section")
    after = (s + 1) % sections
    before = (s + sections - 1) % sections
    partner = sections - 1 - s
    across = (2 * sections - 2 - s) % sections
    sibling = z * 4 + y * 2 + (1 - core)
    other_y = z * 4 + (1 - y) * 2 + core

    def z_of(step):
        return (z + step + 2 * NZ) % NZ

    def dp_of(step):
        return z_of(step) * 4 + y * 2 + core

    def flipped(bit):
        return (y + bit) % 2

    load_slots = pltpu.make_async_copy(pool, slots, local.at[0])
    load_slots.start()
    keep_shard = pltpu.make_async_copy(shard, w.at[d], local.at[1])
    keep_shard.start()

    barrier = pltpu.get_barrier_semaphore()
    for target in (
        (s, sibling),
        (s, other_y),
        (s, dp_of(1)),
        (s, dp_of(-1)),
        (after, d),
        (before, d),
        (partner, d),
    ):
        pl.semaphore_signal(barrier, inc=1, device_id=target, device_id_type=MESH)

    @pl.when(across != s)
    def _():
        pl.semaphore_signal(barrier, inc=1, device_id=(across, d), device_id_type=MESH)
        pl.semaphore_wait(barrier, 8)

    @pl.when(across == s)
    def _():
        pl.semaphore_wait(barrier, 7)

    def gather_copy(i, k, src=None):
        direction, bit, _ = CHAINS[i]
        slot = z_of(-direction * k) * 4 + flipped(bit) * 2 + core
        return remote(
            w.at[slot] if src is None else src,
            w.at[slot],
            ring_send.at[FIRST[i] + k],
            ring_recv.at[FIRST[i] + k],
            s,
            dp_of(direction),
        )

    def gathered(i, k):
        direction, bit, _ = CHAINS[i]
        slot = z_of(-direction * (k + 1)) * 4 + flipped(bit) * 2 + core
        return slot, remote(
            w.at[slot],
            w.at[slot],
            ring_send.at[FIRST[i] + k],
            ring_recv.at[FIRST[i] + k],
            s,
            dp_of(direction),
        )

    def to_sibling(slot, index, src=None):
        return remote(
            w.at[slot] if src is None else src,
            w.at[slot],
            sib_send.at[index],
            sib_recv.at[index],
            s,
            sibling,
        )

    def from_sibling(slot, index):
        other = slot + 1 - 2 * core
        return remote(w.at[other], w.at[other], sib_send.at[index], sib_recv.at[index], s, sibling)

    exchange = remote(shard, w.at[d], y_send.at[0], y_recv.at[0], s, other_y)
    exchange.start()
    sends = [exchange, gather_copy(0, 0, shard), gather_copy(3, 0, shard), to_sibling(d, 14, shard)]
    for copy in sends[1:]:
        copy.start()

    load_slots.wait()
    mine_fetch = plan[s, 0]
    mine_keep = plan[s, 1]
    theirs_fetch = plan[partner, 0]
    theirs_keep = plan[partner, 1]

    def pick(c, carry):
        at = pl.ds(pl.multiple_of(c * CHIP, 128), CHIP)
        first = slots[0, :, at].astype(F32)
        second = slots[1, :, at].astype(F32)
        wanted[:, at] = jnp.where(theirs_fetch >= 3, second, first).astype(BF16)
        return carry

    lax.fori_loop(0, chips, pick, 0)

    def wanted_copy(n):
        at = pl.ds(n * (rows // PIECES), rows // PIECES)
        return remote(wanted.at[at], stash.at[at], wanted_send.at[n], wanted_recv.at[n], partner, d)


    slot_y = z * 4 + (1 - y) * 2 + core
    remote(w.at[slot_y], w.at[slot_y], y_send.at[0], y_recv.at[0], s, other_y).wait_recv()
    for n in range(PIECES):
        wanted_copy(n).start()
    more = [gather_copy(1, 0), gather_copy(2, 0), to_sibling(slot_y, 15)]
    for copy in more:
        copy.start()
    sends += more
    sib_slots = [(d, 14), (slot_y, 15)]
    def gather_round(k):
        for i, (_, _, hops) in enumerate(CHAINS):
            if k >= hops:
                continue
            slot, arrival = gathered(i, k)
            arrival.wait_recv()
            if k + 1 < hops:
                copy = gather_copy(i, k + 1)
                copy.start()
                sends.append(copy)
            copy = to_sibling(slot, FIRST[i] + k)
            copy.start()
            sends.append(copy)
            sib_slots.append((slot, FIRST[i] + k))

    piece = width // PIECES

    def grad_copy(n):
        at = pl.ds(n * piece, piece)
        return remote(grad.at[:, at], up.at[:, at], grad_send.at[n], grad_recv.at[n], before, d)

    def act_copy(n):
        at = pl.ds(n * (rows // SLICES), rows // SLICES)
        return remote(act.at[at], xin.at[at], act_send.at[n], act_recv.at[n], after, d)

    def pin_copy(n):
        at = pl.ds(n * (rows // SLICES), rows // SLICES)
        return remote(act.at[at], pin.at[at], pin_send.at[n], pin_recv.at[n], across, d)

    pin_local = pltpu.make_async_copy(act, pin, local.at[2])

    gather_round(0)
    gather_round(1)
    for n in range(PIECES - 1):
        wanted_copy(n).wait_recv()
    for n in range(PIECES):
        grad_copy(n).start()

    @pl.when(across == s)
    def _():
        pin_local.start()

    gather_round(2)

    def w_in_of(c):
        return jnp.concatenate([w[2 * c, :HALF, :], w[2 * c + 1, :HALF, :]], axis=0)

    def w_out_of(c):
        return jnp.concatenate([w[2 * c, HALF:CHIP, :], w[2 * c + 1, HALF:CHIP, :]], axis=0)

    def gain_of(c):
        both = w[2 * c, CHIP:PACK, :].astype(F32) + w[2 * c + 1, CHIP:PACK, :].astype(F32)
        return both[:1]

    def lanes(c):
        return pl.ds(pl.multiple_of(c * CHIP, 128), CHIP)

    def folded(v):
        return v[:, :128] + v[:, 128:256] + v[:, 256:]

    def stats(ref):
        zero = jnp.zeros((rows, 128), F32)
        total = lax.fori_loop(
            0, chips, lambda c, acc: acc + folded(ref[:, lanes(c)].astype(F32)), zero
        )
        mean = jnp.sum(total, axis=1, keepdims=True) / width

        def spread(c, acc):
            centred = ref[:, lanes(c)].astype(F32) - mean
            return acc + folded(centred * centred)

        total = lax.fori_loop(0, chips, spread, zero)
        inverse = lax.rsqrt(jnp.sum(total, axis=1, keepdims=True) / width + EPSILON)
        return mean, inverse

    wanted_copy(PIECES - 1).wait_recv()

    def choose(c, carry):
        at = lanes(c)
        own = jnp.where(mine_fetch >= 1, slots[1, :, at].astype(F32), slots[0, :, at].astype(F32))
        stash[:, at] = jnp.where(mine_fetch >= 2, stash[:, at].astype(F32), own).astype(BF16)
        return carry

    lax.fori_loop(0, chips, choose, 0)
    mean_z, inverse_z = stats(stash)
    gather_round(3)
    for slot, index in sib_slots:
        from_sibling(slot, index).wait_recv()
    keep_shard.wait()

    def pre_step(c, pre):
        at = lanes(c)
        unit = (stash[:, at].astype(F32) - mean_z) * inverse_z
        rounded = (unit * gain_of(c)).astype(BF16)
        normed[:, at] = rounded
        return pre + jnp.dot(rounded, w_in_of(c), preferred_element_type=F32)

    def d_hidden_step(c, d_hidden):
        return d_hidden + jnp.dot(up[:, lanes(c)], w_out_of(c), preferred_element_type=F32)

    zero = jnp.zeros((rows, CHIP), F32)
    hidden, slope = gelu_and_slope(lax.fori_loop(0, chips, pre_step, zero))
    hidden = hidden.astype(BF16)
    d_hidden = zero
    for n in range(PIECES):
        grad_copy(n).wait_recv()
        first = n * (chips // PIECES)
        d_hidden = lax.fori_loop(first, first + chips // PIECES, d_hidden_step, d_hidden)
    d_pre = (d_hidden * slope).astype(BF16)

    def half_copy(chip):
        return remote(
            part.at[chip, 1 - core],
            sib_part.at[chip],
            half_send.at[chip],
            half_recv.at[chip],
            s,
            sibling,
        )

    def chip_at(i, k):
        direction, bit, hops = CHAINS[i]
        return z_of(direction * (hops - k)) * 2 + flipped(bit)

    entries = [(i, k) for k in range(4) for i in (1, 2, 0, 3) if k < CHAINS[i][2]]
    order = [chip_at(i, k) for i, k in entries]
    own_far = z * 2 + flipped(1)
    own_near = z * 2 + y
    order += [own_far, own_near]

    def partials(chip, row_sums):
        at = lanes(chip)
        rounded = normed[:, at]
        u = up[:, at]
        p_in = lax.dot_general(rounded, d_pre, ROWS_IN_COMMON, preferred_element_type=F32)
        p_out = lax.dot_general(u, hidden, ROWS_IN_COMMON, preferred_element_type=F32)
        p_in = p_in.astype(BF16)
        p_out = p_out.astype(BF16)
        d_normed = lax.dot_general(d_pre, w_in_of(chip), COLS_IN_COMMON, preferred_element_type=F32)
        unit = (stash[:, at].astype(F32) - mean_z) * inverse_z
        p_gain = jnp.sum(d_normed * unit, axis=0, keepdims=True)
        p_gain = jnp.broadcast_to(p_gain, (16, CHIP)).astype(BF16)
        for half in range(2):
            part[chip, half, :HALF, :] = p_in[half * HALF : (half + 1) * HALF]
            part[chip, half, HALF:CHIP, :] = p_out[half * HALF : (half + 1) * HALF]
            part[chip, half, CHIP:PACK, :] = p_gain
        half_copy(chip).start()
        d_u = d_normed * gain_of(chip)
        d_unit[:, at] = d_u
        return row_sums[0] + folded(d_u), row_sums[1] + folded(d_u * unit)

    row_sums = (jnp.zeros((rows, 128), F32), jnp.zeros((rows, 128), F32))

    def chain_copy(i, k):
        return remote(
            part.at[chip_at(i, k), core],
            chain_in.at[FIRST[i] + k],
            chain_send.at[FIRST[i] + k],
            chain_recv.at[FIRST[i] + k],
            s,
            dp_of(CHAINS[i][0]),
        )

    def chip_sum(chip, *arrived):
        half_copy(chip).wait_recv()
        total = part[chip, core].astype(F32) + sib_part[chip].astype(F32)
        for index in arrived:
            total += chain_in[index].astype(F32)
        return total

    def chain_step(i, k):
        chip = chip_at(i, k)
        arrived = ()
        if k > 0:
            chain_copy(i, k - 1).wait_recv()
            arrived = (FIRST[i] + k - 1,)
        part[chip, core] = chip_sum(chip, *arrived).astype(BF16)
        chain_copy(i, k).start()
        n = entries.index((i, k))
        if n in ACT_STEPS:
            act_copy(SLICES - len(ACT_STEPS) + ACT_STEPS.index(n)).start()
        if 6 <= n < 6 + SLICES:

            @pl.when(across != s)
            def _():
                pin_copy(n - 6).start()

    for n, chip in enumerate(order):
        if n % 4 == 0:
            act_copy(n // 4).start()
        row_sums = partials(chip, row_sums)
        if 1 <= n <= 4:
            chain_step(*entries[n - 1])
    for i, k in entries[4:8]:
        chain_step(i, k)

    mean_d = jnp.sum(row_sums[0], axis=1, keepdims=True) / width
    mean_du = jnp.sum(row_sums[1], axis=1, keepdims=True) / width

    def input_grad(c, carry):
        at = lanes(c)
        unit = (stash[:, at].astype(F32) - mean_z) * inverse_z
        change = inverse_z * (d_unit[:, at] - mean_d - unit * mean_du)
        normed[:, at] = (up[:, at].astype(F32) + change).astype(BF16)
        return carry

    lax.fori_loop(0, chips, input_grad, 0)
    store_grad = pltpu.make_async_copy(normed, grad_next, local.at[3])
    store_grad.start()
    for i, k in entries[8:]:
        chain_step(i, k)

    for i in (1, 2):
        chain_copy(i, CHAINS[i][2] - 1).wait_recv()
    part[own_far, core] = chip_sum(
        own_far, FIRST[1] + CHAINS[1][2] - 1, FIRST[2] + CHAINS[2][2] - 1
    ).astype(BF16)
    last_copy = remote(
        part.at[own_far, core], last_in, last_send.at[0], last_recv.at[0], s, other_y
    )
    last_copy.start()

    for n in range(SLICES):
        act_copy(n).wait_recv()
    mean_x, inverse_x = stats(xin)

    def pre_x_step(c, pre_x):
        unit = (xin[:, lanes(c)].astype(F32) - mean_x) * inverse_x
        rounded = (unit * gain_of(c)).astype(BF16)
        return pre_x + jnp.dot(rounded, w_in_of(c), preferred_element_type=F32)

    hidden_x, _ = gelu_and_slope(lax.fori_loop(0, chips, pre_x_step, zero))
    hidden_x = hidden_x.astype(BF16)

    def forward_step(c, carry):
        at = lanes(c)
        added = lax.dot_general(hidden_x, w_out_of(c), COLS_IN_COMMON, preferred_element_type=F32)
        out_act[:, at] = (xin[:, at].astype(F32) + added).astype(BF16)
        return carry

    lax.fori_loop(0, chips, forward_step, 0)
    store_act = pltpu.make_async_copy(out_act, act_next, local.at[4])
    store_act.start()

    @pl.when(across != s)
    def _():
        for n in range(SLICES):
            pin_copy(n).wait()

    @pl.when(across == s)
    def _():
        pin_local.wait()

    def keep(c, carry):
        at = lanes(c)
        for j in range(2):
            value = jnp.where(
                theirs_keep == j + 2, pin[:, at].astype(F32), slots[j, :, at].astype(F32)
            )
            slots[j, :, at] = jnp.where(mine_keep == j, xin[:, at].astype(F32), value).astype(BF16)
        return carry

    lax.fori_loop(0, chips, keep, 0)
    store_pool = pltpu.make_async_copy(slots, pool_next, local.at[5])
    store_pool.start()

    for i in (0, 3):
        chain_copy(i, CHAINS[i][2] - 1).wait_recv()
    total = chip_sum(own_near, FIRST[0] + CHAINS[0][2] - 1, FIRST[3] + CHAINS[3][2] - 1)
    last_copy.wait_recv()
    sums[...] = total + last_in[...].astype(F32)

    for copy in sends:
        copy.wait_send()
    for n in range(PIECES):
        grad_copy(n).wait_send()
        wanted_copy(n).wait_send()
    for n in range(SLICES):
        act_copy(n).wait_send()
    for chip in order:
        half_copy(chip).wait_send()
    for i, k in entries:
        chain_copy(i, k).wait_send()
    last_copy.wait_send()
    store_grad.wait()
    store_act.wait()
    store_pool.wait()


def per_device(act_sent, grad_sent, stash_pool, w_in, w_out, gain, plan):
    rows, width = act_sent.shape[1:]
    core = lax.axis_index("dp") % 2
    gain_row = jnp.tile(gain, (1, 2))
    lane = lax.broadcasted_iota(jnp.int32, gain_row.shape, 1)
    gain_row = jnp.where(lane // HALF == core, gain_row, jnp.zeros_like(gain_row))
    shard = jnp.concatenate(
        [w_in[0], w_out[0].T, jnp.broadcast_to(gain_row, (16, CHIP))], axis=0
    )
    anywhere = pl.BlockSpec(memory_space=pl.ANY)
    vmem = pl.BlockSpec(memory_space=pltpu.VMEM)
    block = jax.ShapeDtypeStruct((rows, width), BF16)
    chips = width // CHIP
    dma = pltpu.SemaphoreType.DMA
    act_next, grad_next, pool_next, sums = pl.pallas_call(
        tick_kernel,
        out_shape=(
            block,
            block,
            jax.ShapeDtypeStruct((2, rows, width), BF16),
            jax.ShapeDtypeStruct((PACK, CHIP), F32),
        ),
        in_specs=[
            vmem,
            pl.BlockSpec(memory_space=pltpu.SMEM),
            anywhere,
            anywhere,
            anywhere,
        ],
        out_specs=(anywhere, anywhere, anywhere, vmem),
        scratch_shapes=[
            pltpu.VMEM((2 * chips, PACK, CHIP), BF16),
            pltpu.VMEM((chips, 2, PACK, CHIP), BF16),
            pltpu.VMEM((chips, PACK, CHIP), BF16),
            pltpu.VMEM((STEPS, PACK, CHIP), BF16),
            pltpu.VMEM((PACK, CHIP), BF16),
            pltpu.VMEM((2, rows, width), BF16),
            pltpu.VMEM((rows, width), BF16),
            pltpu.VMEM((rows, width), BF16),
            pltpu.VMEM((rows, width), BF16),
            pltpu.VMEM((rows, width), BF16),
            pltpu.VMEM((rows, width), BF16),
            pltpu.VMEM((rows, width), BF16),
            pltpu.VMEM((rows, width), F32),
            pltpu.VMEM((rows, width), BF16),
            dma((STEPS,)),
            dma((STEPS,)),
            dma((16,)),
            dma((16,)),
            dma((1,)),
            dma((1,)),
            dma((PIECES,)),
            dma((PIECES,)),
            dma((PIECES,)),
            dma((PIECES,)),
            dma((SLICES,)),
            dma((SLICES,)),
            dma((SLICES,)),
            dma((SLICES,)),
            dma((STEPS,)),
            dma((STEPS,)),
            dma((chips,)),
            dma((chips,)),
            dma((1,)),
            dma((1,)),
            dma((6,)),
        ],
        compiler_params=pltpu.CompilerParams(
            collective_id=0, has_side_effects=True, vmem_limit_bytes=60 * 1024 * 1024
        ),
        cost_estimate=pl.CostEstimate(
            flops=14 * rows * width * CHIP, bytes_accessed=20 * rows * width, transcendentals=0
        ),
    )(shard, plan, act_sent[0], grad_sent[0], stash_pool[0])
    sum_gain = lax.dynamic_slice_in_dim(sums[CHIP], core * HALF, HALF)
    return (
        act_next[None],
        grad_next[None],
        pool_next[None],
        sums[None, :HALF],
        sums[HALF:CHIP].T[None],
        sum_gain[None],
    )


def solution(mesh):
    placed = (
        P("section", "dp", None),
        P("section", "dp", None),
        P("section", None, "dp", None),
        P("section", "dp", None),
        P("section", None, "dp"),
        P("section", "dp"),
        P(),
    )
    return jax.shard_map(
        per_device,
        mesh=mesh,
        in_specs=placed,
        out_specs=(
            P("section", "dp", None),
            P("section", "dp", None),
            P("section", None, "dp", None),
            P("section", "dp", None),
            P("section", None, "dp"),
            P("section", "dp"),
        ),
        check_vma=False,
    )
```

```python
import jax
import jax.numpy as jnp
from jax import lax
from jax.experimental import pallas as pl
from jax.experimental.pallas import tpu as pltpu
from jax.sharding import PartitionSpec as P

EPSILON = 1e-05
MESH = pl.DeviceIdType.MESH
F32 = jnp.float32
BF16 = jnp.bfloat16
ROWS_IN_COMMON = (((0,), (0,)), ((), ()))
COLS_IN_COMMON = (((1,), (1,)), ((), ()))

NZ = 8
HALF = 192
CHIP = 2 * HALF
PACK = 2 * HALF + 16

CHAINS = ((1, 0, 4), (-1, 1, 4), (1, 1, 3), (-1, 0, 3))
FIRST = (0, 4, 8, 11)
STEPS = 14
ACT_STEPS = (4, 6)
SLICES = 8
PIECES = 4


def remote(src, dst, send_sem, recv_sem, section, dp):
    return pltpu.make_async_remote_copy(
        src_ref=src,
        dst_ref=dst,
        send_sem=send_sem,
        recv_sem=recv_sem,
        device_id=(section, dp),
        device_id_type=MESH,
    )


def gelu_and_slope(x):
    c = 0.7978845608028654
    a = 0.044715
    t = jnp.tanh(c * (x + a * (x * x * x)))
    hidden = x * (0.5 * (1.0 + t))
    slope = 0.5 * (1.0 + t) + 0.5 * x * (1.0 - t * t) * (c * (1.0 + 3.0 * a * (x * x)))
    return hidden, slope


def tick_kernel(
    shard,
    plan,
    act,
    grad,
    pool,
    act_next,
    grad_next,
    pool_next,
    sums,
    w,
    part,
    sib_part,
    chain_in,
    last_in,
    slots,
    wanted,
    stash,
    up,
    xin,
    pin,
    normed,
    d_unit,
    out_act,
    ring_send,
    ring_recv,
    sib_send,
    sib_recv,
    y_send,
    y_recv,
    grad_send,
    grad_recv,
    wanted_send,
    wanted_recv,
    act_send,
    act_recv,
    pin_send,
    pin_recv,
    chain_send,
    chain_recv,
    half_send,
    half_recv,
    last_send,
    last_recv,
    local,
):
    rows, width = act.shape
    chips = width // CHIP
    s = lax.axis_index("section")
    d = lax.axis_index("dp")
    core = d % 2
    y = (d // 2) % 2
    z = d // 4
    sections = lax.axis_size("section")
    after = (s + 1) % sections
    before = (s + sections - 1) % sections
    partner = sections - 1 - s
    across = (2 * sections - 2 - s) % sections
    sibling = z * 4 + y * 2 + (1 - core)
    other_y = z * 4 + (1 - y) * 2 + core

    def z_of(step):
        return (z + step + 2 * NZ) % NZ

    def dp_of(step):
        return z_of(step) * 4 + y * 2 + core

    def flipped(bit):
        return (y + bit) % 2

    load_slots = pltpu.make_async_copy(pool, slots, local.at[0])
    load_slots.start()
    keep_shard = pltpu.make_async_copy(shard, w.at[d], local.at[1])
    keep_shard.start()

    barrier = pltpu.get_barrier_semaphore()
    for target in (
        (s, sibling),
        (s, other_y),
        (s, dp_of(1)),
        (s, dp_of(-1)),
        (after, d),
        (before, d),
        (partner, d),
    ):
        pl.semaphore_signal(barrier, inc=1, device_id=target, device_id_type=MESH)

    @pl.when(across != s)
    def _():
        pl.semaphore_signal(barrier, inc=1, device_id=(across, d), device_id_type=MESH)
        pl.semaphore_wait(barrier, 8)

    @pl.when(across == s)
    def _():
        pl.semaphore_wait(barrier, 7)

    def gather_copy(i, k, src=None):
        direction, bit, _ = CHAINS[i]
        slot = z_of(-direction * k) * 4 + flipped(bit) * 2 + core
        return remote(
            w.at[slot] if src is None else src,
            w.at[slot],
            ring_send.at[FIRST[i] + k],
            ring_recv.at[FIRST[i] + k],
            s,
            dp_of(direction),
        )

    def gathered(i, k):
        direction, bit, _ = CHAINS[i]
        slot = z_of(-direction * (k + 1)) * 4 + flipped(bit) * 2 + core
        return slot, remote(
            w.at[slot],
            w.at[slot],
            ring_send.at[FIRST[i] + k],
            ring_recv.at[FIRST[i] + k],
            s,
            dp_of(direction),
        )

    def to_sibling(slot, index, src=None):
        return remote(
            w.at[slot] if src is None else src,
            w.at[slot],
            sib_send.at[index],
            sib_recv.at[index],
            s,
            sibling,
        )

    def from_sibling(slot, index):
        other = slot + 1 - 2 * core
        return remote(w.at[other], w.at[other], sib_send.at[index], sib_recv.at[index], s, sibling)

    exchange = remote(shard, w.at[d], y_send.at[0], y_recv.at[0], s, other_y)
    exchange.start()
    sends = [exchange, gather_copy(0, 0, shard), gather_copy(3, 0, shard), to_sibling(d, 14, shard)]
    for copy in sends[1:]:
        copy.start()

    load_slots.wait()
    mine_fetch = plan[s, 0]
    mine_keep = plan[s, 1]
    theirs_fetch = plan[partner, 0]
    theirs_keep = plan[partner, 1]

    def pick(c, carry):
        at = pl.ds(pl.multiple_of(c * CHIP, 128), CHIP)
        first = slots[0, :, at].astype(F32)
        second = slots[1, :, at].astype(F32)
        wanted[:, at] = jnp.where(theirs_fetch >= 3, second, first).astype(BF16)
        return carry

    lax.fori_loop(0, chips, pick, 0)

    def wanted_copy(n):
        at = pl.ds(n * (rows // PIECES), rows // PIECES)
        return remote(wanted.at[at], stash.at[at], wanted_send.at[n], wanted_recv.at[n], partner, d)


    slot_y = z * 4 + (1 - y) * 2 + core
    remote(w.at[slot_y], w.at[slot_y], y_send.at[0], y_recv.at[0], s, other_y).wait_recv()
    for n in range(PIECES):
        wanted_copy(n).start()
    more = [gather_copy(1, 0), gather_copy(2, 0), to_sibling(slot_y, 15)]
    for copy in more:
        copy.start()
    sends += more
    sib_slots = [(d, 14), (slot_y, 15)]
    def gather_round(k):
        for i, (_, _, hops) in enumerate(CHAINS):
            if k >= hops:
                continue
            slot, arrival = gathered(i, k)
            arrival.wait_recv()
            if k + 1 < hops:
                copy = gather_copy(i, k + 1)
                copy.start()
                sends.append(copy)
            copy = to_sibling(slot, FIRST[i] + k)
            copy.start()
            sends.append(copy)
            sib_slots.append((slot, FIRST[i] + k))

    piece = width // PIECES

    def grad_copy(n):
        at = pl.ds(n * piece, piece)
        return remote(grad.at[:, at], up.at[:, at], grad_send.at[n], grad_recv.at[n], before, d)

    def act_copy(n):
        at = pl.ds(n * (rows // SLICES), rows // SLICES)
        return remote(act.at[at], xin.at[at], act_send.at[n], act_recv.at[n], after, d)

    def pin_copy(n):
        at = pl.ds(n * (rows // SLICES), rows // SLICES)
        return remote(act.at[at], pin.at[at], pin_send.at[n], pin_recv.at[n], across, d)

    pin_local = pltpu.make_async_copy(act, pin, local.at[2])

    gather_round(0)
    gather_round(1)
    for n in range(PIECES - 1):
        wanted_copy(n).wait_recv()
    for n in range(PIECES):
        grad_copy(n).start()

    @pl.when(across == s)
    def _():
        pin_local.start()

    gather_round(2)

    def w_in_of(c):
        return jnp.concatenate([w[2 * c, :HALF, :], w[2 * c + 1, :HALF, :]], axis=0)

    def w_out_of(c):
        return jnp.concatenate([w[2 * c, HALF:CHIP, :], w[2 * c + 1, HALF:CHIP, :]], axis=0)

    def gain_of(c):
        both = w[2 * c, CHIP:PACK, :].astype(F32) + w[2 * c + 1, CHIP:PACK, :].astype(F32)
        return both[:1]

    def lanes(c):
        return pl.ds(pl.multiple_of(c * CHIP, 128), CHIP)

    def folded(v):
        return v[:, :128] + v[:, 128:256] + v[:, 256:]

    def stats(ref):
        zero = jnp.zeros((rows, 128), F32)
        total = lax.fori_loop(
            0, chips, lambda c, acc: acc + folded(ref[:, lanes(c)].astype(F32)), zero
        )
        mean = jnp.sum(total, axis=1, keepdims=True) / width

        def spread(c, acc):
            centred = ref[:, lanes(c)].astype(F32) - mean
            return acc + folded(centred * centred)

        total = lax.fori_loop(0, chips, spread, zero)
        inverse = lax.rsqrt(jnp.sum(total, axis=1, keepdims=True) / width + EPSILON)
        return mean, inverse

    wanted_copy(PIECES - 1).wait_recv()

    def choose(c, carry):
        at = lanes(c)
        own = jnp.where(mine_fetch >= 1, slots[1, :, at].astype(F32), slots[0, :, at].astype(F32))
        stash[:, at] = jnp.where(mine_fetch >= 2, stash[:, at].astype(F32), own).astype(BF16)
        return carry

    lax.fori_loop(0, chips, choose, 0)
    mean_z, inverse_z = stats(stash)
    gather_round(3)
    for slot, index in sib_slots:
        from_sibling(slot, index).wait_recv()
    keep_shard.wait()

    def pre_step(c, pre):
        at = lanes(c)
        unit = (stash[:, at].astype(F32) - mean_z) * inverse_z
        rounded = (unit * gain_of(c)).astype(BF16)
        normed[:, at] = rounded
        return pre + jnp.dot(rounded, w_in_of(c), preferred_element_type=F32)

    def d_hidden_step(c, d_hidden):
        return d_hidden + jnp.dot(up[:, lanes(c)], w_out_of(c), preferred_element_type=F32)

    zero = jnp.zeros((rows, CHIP), F32)
    hidden, slope = gelu_and_slope(lax.fori_loop(0, chips, pre_step, zero))
    hidden = hidden.astype(BF16)
    d_hidden = zero
    for n in range(PIECES):
        grad_copy(n).wait_recv()
        if n >= 2:
            act_copy(n - 2).start()
        first = n * (chips // PIECES)
        d_hidden = lax.fori_loop(first, first + chips // PIECES, d_hidden_step, d_hidden)
    d_pre = (d_hidden * slope).astype(BF16)

    def half_copy(chip):
        return remote(
            part.at[chip, 1 - core],
            sib_part.at[chip],
            half_send.at[chip],
            half_recv.at[chip],
            s,
            sibling,
        )

    def chip_at(i, k):
        direction, bit, hops = CHAINS[i]
        return z_of(direction * (hops - k)) * 2 + flipped(bit)

    entries = [(i, k) for k in range(4) for i in (1, 2, 0, 3) if k < CHAINS[i][2]]
    order = [chip_at(i, k) for i, k in entries]
    own_far = z * 2 + flipped(1)
    own_near = z * 2 + y
    order += [own_far, own_near]

    def partials(chip, row_sums):
        at = lanes(chip)
        rounded = normed[:, at]
        u = up[:, at]
        p_in = lax.dot_general(rounded, d_pre, ROWS_IN_COMMON, preferred_element_type=F32)
        p_out = lax.dot_general(u, hidden, ROWS_IN_COMMON, preferred_element_type=F32)
        p_in = p_in.astype(BF16)
        p_out = p_out.astype(BF16)
        d_normed = lax.dot_general(d_pre, w_in_of(chip), COLS_IN_COMMON, preferred_element_type=F32)
        unit = (stash[:, at].astype(F32) - mean_z) * inverse_z
        p_gain = jnp.sum(d_normed * unit, axis=0, keepdims=True)
        p_gain = jnp.broadcast_to(p_gain, (16, CHIP)).astype(BF16)
        for half in range(2):
            part[chip, half, :HALF, :] = p_in[half * HALF : (half + 1) * HALF]
            part[chip, half, HALF:CHIP, :] = p_out[half * HALF : (half + 1) * HALF]
            part[chip, half, CHIP:PACK, :] = p_gain
        half_copy(chip).start()
        d_u = d_normed * gain_of(chip)
        d_unit[:, at] = d_u
        return row_sums[0] + folded(d_u), row_sums[1] + folded(d_u * unit)

    row_sums = (jnp.zeros((rows, 128), F32), jnp.zeros((rows, 128), F32))

    def chain_copy(i, k):
        return remote(
            part.at[chip_at(i, k), core],
            chain_in.at[FIRST[i] + k],
            chain_send.at[FIRST[i] + k],
            chain_recv.at[FIRST[i] + k],
            s,
            dp_of(CHAINS[i][0]),
        )

    def chip_sum(chip, *arrived):
        half_copy(chip).wait_recv()
        total = part[chip, core].astype(F32) + sib_part[chip].astype(F32)
        for index in arrived:
            total += chain_in[index].astype(F32)
        return total

    def chain_step(i, k):
        chip = chip_at(i, k)
        arrived = ()
        if k > 0:
            chain_copy(i, k - 1).wait_recv()
            arrived = (FIRST[i] + k - 1,)
        part[chip, core] = chip_sum(chip, *arrived).astype(BF16)
        chain_copy(i, k).start()
        n = entries.index((i, k))
        if n in ACT_STEPS:
            act_copy(SLICES - len(ACT_STEPS) + ACT_STEPS.index(n)).start()
        if 6 <= n < 6 + SLICES:

            @pl.when(across != s)
            def _():
                pin_copy(n - 6).start()

    for n, chip in enumerate(order):
        if n in (3, 7, 11, 15):
            act_copy(2 + n // 4).start()
        row_sums = partials(chip, row_sums)
        if 1 <= n <= 4:
            chain_step(*entries[n - 1])
    for i, k in entries[4:8]:
        chain_step(i, k)

    mean_d = jnp.sum(row_sums[0], axis=1, keepdims=True) / width
    mean_du = jnp.sum(row_sums[1], axis=1, keepdims=True) / width

    def input_grad(c, carry):
        at = lanes(c)
        unit = (stash[:, at].astype(F32) - mean_z) * inverse_z
        change = inverse_z * (d_unit[:, at] - mean_d - unit * mean_du)
        normed[:, at] = (up[:, at].astype(F32) + change).astype(BF16)
        return carry

    lax.fori_loop(0, chips, input_grad, 0)
    store_grad = pltpu.make_async_copy(normed, grad_next, local.at[3])
    store_grad.start()
    for i, k in entries[8:]:
        chain_step(i, k)

    for i in (1, 2):
        chain_copy(i, CHAINS[i][2] - 1).wait_recv()
    part[own_far, core] = chip_sum(
        own_far, FIRST[1] + CHAINS[1][2] - 1, FIRST[2] + CHAINS[2][2] - 1
    ).astype(BF16)
    last_copy = remote(
        part.at[own_far, core], last_in, last_send.at[0], last_recv.at[0], s, other_y
    )
    last_copy.start()

    for n in range(SLICES):
        act_copy(n).wait_recv()
    mean_x, inverse_x = stats(xin)

    def pre_x_step(c, pre_x):
        unit = (xin[:, lanes(c)].astype(F32) - mean_x) * inverse_x
        rounded = (unit * gain_of(c)).astype(BF16)
        return pre_x + jnp.dot(rounded, w_in_of(c), preferred_element_type=F32)

    hidden_x, _ = gelu_and_slope(lax.fori_loop(0, chips, pre_x_step, zero))
    hidden_x = hidden_x.astype(BF16)

    def forward_step(c, carry):
        at = lanes(c)
        added = lax.dot_general(hidden_x, w_out_of(c), COLS_IN_COMMON, preferred_element_type=F32)
        out_act[:, at] = (xin[:, at].astype(F32) + added).astype(BF16)
        return carry

    lax.fori_loop(0, chips, forward_step, 0)
    store_act = pltpu.make_async_copy(out_act, act_next, local.at[4])
    store_act.start()

    @pl.when(across != s)
    def _():
        for n in range(SLICES):
            pin_copy(n).wait()

    @pl.when(across == s)
    def _():
        pin_local.wait()

    def keep(c, carry):
        at = lanes(c)
        for j in range(2):
            value = jnp.where(
                theirs_keep == j + 2, pin[:, at].astype(F32), slots[j, :, at].astype(F32)
            )
            slots[j, :, at] = jnp.where(mine_keep == j, xin[:, at].astype(F32), value).astype(BF16)
        return carry

    lax.fori_loop(0, chips, keep, 0)
    store_pool = pltpu.make_async_copy(slots, pool_next, local.at[5])
    store_pool.start()

    for i in (0, 3):
        chain_copy(i, CHAINS[i][2] - 1).wait_recv()
    total = chip_sum(own_near, FIRST[0] + CHAINS[0][2] - 1, FIRST[3] + CHAINS[3][2] - 1)
    last_copy.wait_recv()
    sums[...] = total + last_in[...].astype(F32)

    for copy in sends:
        copy.wait_send()
    for n in range(PIECES):
        grad_copy(n).wait_send()
        wanted_copy(n).wait_send()
    for n in range(SLICES):
        act_copy(n).wait_send()
    for chip in order:
        half_copy(chip).wait_send()
    for i, k in entries:
        chain_copy(i, k).wait_send()
    last_copy.wait_send()
    store_grad.wait()
    store_act.wait()
    store_pool.wait()


def per_device(act_sent, grad_sent, stash_pool, w_in, w_out, gain, plan):
    rows, width = act_sent.shape[1:]
    core = lax.axis_index("dp") % 2
    gain_row = jnp.tile(gain, (1, 2))
    lane = lax.broadcasted_iota(jnp.int32, gain_row.shape, 1)
    gain_row = jnp.where(lane // HALF == core, gain_row, jnp.zeros_like(gain_row))
    shard = jnp.concatenate(
        [w_in[0], w_out[0].T, jnp.broadcast_to(gain_row, (16, CHIP))], axis=0
    )
    anywhere = pl.BlockSpec(memory_space=pl.ANY)
    vmem = pl.BlockSpec(memory_space=pltpu.VMEM)
    block = jax.ShapeDtypeStruct((rows, width), BF16)
    chips = width // CHIP
    dma = pltpu.SemaphoreType.DMA
    act_next, grad_next, pool_next, sums = pl.pallas_call(
        tick_kernel,
        out_shape=(
            block,
            block,
            jax.ShapeDtypeStruct((2, rows, width), BF16),
            jax.ShapeDtypeStruct((PACK, CHIP), F32),
        ),
        in_specs=[
            vmem,
            pl.BlockSpec(memory_space=pltpu.SMEM),
            anywhere,
            anywhere,
            anywhere,
        ],
        out_specs=(anywhere, anywhere, anywhere, vmem),
        scratch_shapes=[
            pltpu.VMEM((2 * chips, PACK, CHIP), BF16),
            pltpu.VMEM((chips, 2, PACK, CHIP), BF16),
            pltpu.VMEM((chips, PACK, CHIP), BF16),
            pltpu.VMEM((STEPS, PACK, CHIP), BF16),
            pltpu.VMEM((PACK, CHIP), BF16),
            pltpu.VMEM((2, rows, width), BF16),
            pltpu.VMEM((rows, width), BF16),
            pltpu.VMEM((rows, width), BF16),
            pltpu.VMEM((rows, width), BF16),
            pltpu.VMEM((rows, width), BF16),
            pltpu.VMEM((rows, width), BF16),
            pltpu.VMEM((rows, width), BF16),
            pltpu.VMEM((rows, width), F32),
            pltpu.VMEM((rows, width), BF16),
            dma((STEPS,)),
            dma((STEPS,)),
            dma((16,)),
            dma((16,)),
            dma((1,)),
            dma((1,)),
            dma((PIECES,)),
            dma((PIECES,)),
            dma((PIECES,)),
            dma((PIECES,)),
            dma((SLICES,)),
            dma((SLICES,)),
            dma((SLICES,)),
            dma((SLICES,)),
            dma((STEPS,)),
            dma((STEPS,)),
            dma((chips,)),
            dma((chips,)),
            dma((1,)),
            dma((1,)),
            dma((6,)),
        ],
        compiler_params=pltpu.CompilerParams(
            collective_id=0, has_side_effects=True, vmem_limit_bytes=60 * 1024 * 1024
        ),
        cost_estimate=pl.CostEstimate(
            flops=14 * rows * width * CHIP, bytes_accessed=20 * rows * width, transcendentals=0
        ),
    )(shard, plan, act_sent[0], grad_sent[0], stash_pool[0])
    sum_gain = lax.dynamic_slice_in_dim(sums[CHIP], core * HALF, HALF)
    return (
        act_next[None],
        grad_next[None],
        pool_next[None],
        sums[None, :HALF],
        sums[HALF:CHIP].T[None],
        sum_gain[None],
    )


def solution(mesh):
    placed = (
        P("section", "dp", None),
        P("section", "dp", None),
        P("section", None, "dp", None),
        P("section", "dp", None),
        P("section", None, "dp"),
        P("section", "dp"),
        P(),
    )
    return jax.shard_map(
        per_device,
        mesh=mesh,
        in_specs=placed,
        out_specs=(
            P("section", "dp", None),
            P("section", "dp", None),
            P("section", None, "dp", None),
            P("section", "dp", None),
            P("section", None, "dp"),
            P("section", "dp"),
        ),
        check_vma=False,
    )
```
